128 devices in a mesh: leaf: 4 (over y), row: 32 (over x, z, core).
Axes of the slice: x: 4, y: 4, z: 4, core: 2. Of those that a mesh axis runs over, the one named last changes fastest.
Arguments:
- rhs_sub: float32 [4, 2, 1024, 512], P('leaf', None, 'row'), may hold values from -6 to 6
- rhs_anc: float32 [16384, 512], P('row'), may hold values from -6 to 6
- inv_sub: float32 [4, 2, 1024, 1024], P('leaf', None, 'row'), may hold values from -3 to 3, as said below
- panel_mid: float32 [4, 1024, 1024], P('leaf', 'row'), may hold values from -0.1875 to 0.1875
- panel_anc: float32 [4, 2, 16384, 1024], P('leaf', None, 'row'), may hold values from -0.125 to 0.125
- block_mask: int32 [4, 2, 128], P('leaf', None, 'row'), may hold values 0 or 1
- inv_anc: float32 [16384, 1024], P('row'), may hold values from -3 to 3, as said below
Outputs:
- x_sub: float32 [4, 2, 1024, 512], P('leaf', None, 'row')
- x_anc: float32 [16384, 512], P('row')
The draws below stay inside these ranges and needn't reach their ends.
Inputs may be any that keep to these rules, and one draw needn't show every extreme that they name: `inv_sub`: each [1024, 1024] block is lower triangular with its diagonal between 0.3 and 3. `inv_anc`: each block of 1024 rows has its diagonal between 0.3 and 3.
All inputs are finite; a program needn't handle non-finite values. No bound on the sum of `block_mask` on one device may be relied on, other than what follows from the above.
Results may differ from the reference program's by a relative error of at most 0.00012.
Values sent between devices are 32-bit elements; how exact they have to be, the bound alone decides.
A program may use at most 64 MiB of HBM per device.

```python
import jax
import jax.numpy as jnp
from jax import lax

W = 1024
ANC = 16384
BR = 128
R = 512
GRIDS = 4


def lower_noise(key, shape):
    return jax.random.normal(key, shape, jnp.float32) * (0.5 / jnp.sqrt(W * 1.0))


def diagonal_draw(key, shape):
    return jnp.exp(jax.random.uniform(key, shape, jnp.float32, jnp.log(0.5), jnp.log(2.0)))


def draw_inv_sub(key, part):
    key_noise, key_diag = jax.random.split(jax.random.fold_in(key, 11))
    noise = jnp.tril(lower_noise(key_noise, (GRIDS, 2, W, W)), -1)
    diagonal = diagonal_draw(key_diag, (GRIDS, 2, W))
    return noise + diagonal[..., None] * jnp.eye(W, dtype=jnp.float32)


def draw_inv_anc(key, part):
    key_noise, key_diag = jax.random.split(jax.random.fold_in(key, 23))
    noise = lower_noise(key_noise, (ANC, W))
    diagonal = diagonal_draw(key_diag, (ANC, 1))
    local_row = (jnp.arange(ANC) % W)[:, None]
    column = jnp.arange(W)[None, :]
    return jnp.where(column != local_row, noise, 0.0) + jnp.where(column == local_row, diagonal, 0.0)


def touch_ends(result, rng, smallest, top_value):
    place = [jax.random.randint(jax.random.fold_in(rng, axis), (), 0, length) for axis, length in enumerate(result.shape)]
    longest = result.shape.index(max(result.shape))
    neighbour = place[:longest] + [(place[longest] + 1) % result.shape[longest]] + place[longest + 1:]
    return result.at[tuple(place)].set(smallest).at[tuple(neighbour)].set(top_value)


def levels(key, extent, shards, least, top_value):
    def one(position, parts):
        steps = jax.random.uniform(jax.random.fold_in(jax.random.fold_in(key, 6), position), (parts,), jnp.float32, least / len(shards), top_value / len(shards))
        return jnp.repeat(jnp.exp(steps), extent[position] // parts).reshape((-1,) + (1,) * (len(extent) - position - 1))

    factor_of = one(*shards[0])
    for cut in shards[1:]:
        factor_of = factor_of * one(*cut)
    return factor_of


def scatter_about(key, shape, scale, reach, cuts=(), held_as=jnp.bfloat16):
    level = levels(key, shape, cuts, -0.22, 0.18) if cuts else 1.0
    entries = jax.random.normal(key, shape, jnp.float32) * scale * level
    return jnp.minimum(jnp.maximum(entries, -reach), reach).astype(held_as)


def setup_inputs(seed: int = 0) -> dict:
    keys = jax.random.split(jax.random.key(seed), 8)
    rhs_sub = scatter_about(keys[0], (GRIDS, 2, W, R), 1.0, 6.0, ((0, 4), (2, 32)), jnp.float32)
    rhs_anc = scatter_about(keys[1], (ANC, R), 1.0, 6.0, ((0, 32),), jnp.float32)
    inv_sub = draw_inv_sub(jax.random.fold_in(keys[7], 71), 0)
    panel_mid = scatter_about(keys[3], (GRIDS, W, W), W ** -0.5, 0.1875, ((0, 4), (1, 32)), jnp.float32)
    panel_anc = scatter_about(keys[4], (GRIDS, 2, ANC, W), (2 * W) ** -0.5, 0.125, ((0, 4), (2, 32)), jnp.float32)
    block_mask = touch_ends((jax.random.randint(keys[5], (GRIDS, 2, ANC // BR), 0, 4) < 3).astype(jnp.int32), jax.random.fold_in(keys[5], 1), 0, 1)
    inv_anc = draw_inv_anc(jax.random.fold_in(keys[7], 71), 0)
    return {"rhs_sub": rhs_sub, "rhs_anc": rhs_anc, "inv_sub": inv_sub, "panel_mid": panel_mid, "panel_anc": panel_anc, "block_mask": block_mask, "inv_anc": inv_anc}


def product(left, right):
    return jnp.dot(left, right, precision=lax.Precision.HIGHEST, preferred_element_type=jnp.float32)


def reference(rhs_sub, rhs_anc, inv_sub, panel_mid, panel_anc, block_mask, inv_anc):
    mask_rows = jnp.repeat(block_mask, BR, axis=2).astype(jnp.float32)
    panels = panel_anc * mask_rows[..., None]
    update = jnp.zeros((ANC, R), jnp.float32)
    solved = []
    for grid in range(GRIDS):
        first = product(inv_sub[grid, 0], rhs_sub[grid, 0])
        second = product(inv_sub[grid, 1], rhs_sub[grid, 1] - product(panel_mid[grid], first))
        update = update + product(panels[grid, 0], first) + product(panels[grid, 1], second)
        solved.append((first, second))
    blocks = inv_anc.reshape(ANC // W, W, W)
    values = (rhs_anc - update).reshape(ANC // W, W, R)
    forward = jnp.einsum("kij,kjr->kir", blocks, values, precision=lax.Precision.HIGHEST)
    x_anc = jnp.einsum("kji,kjr->kir", blocks, forward, precision=lax.Precision.HIGHEST).reshape(ANC, R)
    outputs = []
    for grid in range(GRIDS):
        first, second = solved[grid]
        x_second = product(inv_sub[grid, 1].T, second - product(panels[grid, 1].T, x_anc))
        x_first = product(inv_sub[grid, 0].T, first - product(panel_mid[grid].T, x_second) - product(panels[grid, 0].T, x_anc))
        outputs.append(jnp.stack([x_first, x_second]))
    return jnp.stack(outputs), x_anc
```

```python
import functools

import jax
import jax.numpy as jnp
from jax import lax
from jax.experimental import pallas as pl
from jax.experimental.pallas import tpu as pltpu
from jax.sharding import PartitionSpec as P

F32 = jnp.float32
BF16 = jnp.bfloat16
MESH = pl.DeviceIdType.MESH
COPIES = 192


def split(value):
    high = value.astype(BF16)
    return high, (value - high.astype(F32)).astype(BF16)


def dot(left, right):
    return jnp.dot(left, right, preferred_element_type=F32)


def product(left, right):
    left_high, left_low = left
    right_high, right_low = right
    return dot(left_high, right_high) + (dot(left_high, right_low) + dot(left_low, right_high))


def kernel(
    rhs_sub, rhs_anc, inv_sub, panel_mid, panel_anc, mask, inv_anc,
    x_sub, x_anc,
    rhs0, rhs1, inv0, inv1, mid, panels, anc, anc_rhs,
    tee, first, second, op_high, op_low, first_high, first_low,
    update, y_in, value, fwd_t, x_t, x_out, z_t, w_t,
    w_send, r_first, r_sum, r_second, out_sub, mask_tile,
    send_sem, recv_sem, local_sem,
):
    y = lax.axis_index("leaf")
    r = lax.axis_index("row")
    x, z, c = r // 8, (r // 2) % 4, r % 2
    o = 1 - c

    def at_x(d):
        return (y, ((x + d) % 4) * 8 + z * 2 + c)

    def at_z(d):
        return (y, x * 8 + ((z + d) % 4) * 2 + c)

    def at_y(d):
        return ((y + d) % 4, r)

    sibling = (y, x * 8 + z * 2 + o)

    count = [0, 0]
    sends = []

    def remote(src, dst, landing, device):
        index = count[0]
        count[0] += 1
        out = pltpu.make_async_remote_copy(
            src_ref=src, dst_ref=dst, send_sem=send_sem.at[index], recv_sem=recv_sem.at[index],
            device_id=device, device_id_type=MESH,
        )
        out.start()
        sends.append(out)
        into = pltpu.make_async_remote_copy(
            src_ref=landing, dst_ref=landing, send_sem=send_sem.at[index], recv_sem=recv_sem.at[index],
            device_id=device, device_id_type=MESH,
        )
        return into.wait_recv

    def local(src, dst):
        index = count[1]
        count[1] += 1
        copy = pltpu.make_async_copy(src, dst, local_sem.at[index])
        copy.start()
        return copy.wait

    def wait_all(waits):
        for wait in waits:
            wait()

    def columns(core, half):
        return pl.ds(pl.multiple_of(core * 256 + half * 128, 128), 128)

    mine = pl.ds(pl.multiple_of(c * 32, 32), 32)
    theirs = pl.ds(pl.multiple_of(o * 32, 32), 32)

    load_rhs = []
    for h in range(2):
        load_rhs.append(local(rhs_sub.at[0, 0, :, columns(c, h)], rhs0.at[h, x, z, mine]))
    load_inv0 = [local(inv_sub.at[0, 0, pl.ds(16 * h, 16)], inv0.at[x, z, c, h]) for h in range(2)]
    load_mid = [local(panel_mid.at[0, pl.ds(16 * h, 16)], mid.at[x, z, c, h]) for h in range(2)]
    load_rhs1 = [local(rhs_sub.at[0, 1, :, columns(c, h)], rhs1.at[h, mine]) for h in range(2)]
    load_inv1 = [local(inv_sub.at[0, 1, pl.ds(16 * h, 16)], inv1.at[x, z, c, h]) for h in range(2)]
    load_panels = [local(panel_anc.at[0, s], panels.at[s, c]) for s in range(2)]
    both = pl.ds(pl.multiple_of(c * 256, 256), 256)
    other = pl.ds(pl.multiple_of(o * 256, 256), 256)
    load_anc = [local(inv_anc, anc.at[c]), local(rhs_anc.at[:, both], anc_rhs.at[c])]
    for s in range(2):
        for j in range(4):
            mask_tile[c, s, j] = jnp.full((8, 128), mask[0, s, j].astype(F32), F32)

    barrier = pltpu.get_barrier_semaphore()
    for device in [at_x(1), at_x(2), at_x(3), at_z(1), at_z(2), at_z(3), at_y(1), at_y(2), at_y(3), sibling]:
        pl.semaphore_signal(barrier, inc=1, device_id=device, device_id_type=MESH)
    pl.semaphore_wait(barrier, 10)

    swap_rhs0 = [
        remote(rhs_sub.at[0, 0, :, columns(o, h)], rhs0.at[h, x, z, mine], rhs0.at[h, x, z, theirs], sibling)
        for h in range(2)
    ]
    swap_rhs1 = [
        remote(rhs_sub.at[0, 1, :, columns(o, h)], rhs1.at[h, mine], rhs1.at[h, theirs], sibling)
        for h in range(2)
    ]
    swap_mask = [remote(mask_tile.at[c], mask_tile.at[c], mask_tile.at[o], sibling)]

    def vector_one(ref):
        along_z = [remote(ref.at[0, x, z], ref.at[0, x, z], ref.at[0, x, (z - d) % 4], at_z(d)) for d in (1, 3, 2)]
        along_x = [remote(ref.at[1, x, z], ref.at[1, x, z], ref.at[1, (x - d) % 4, z], at_x(d)) for d in (1, 3, 2)]
        return along_z, along_x

    def vector_two(ref, waits):
        along_z, along_x = waits
        wait_all(along_z)
        then_x = [remote(ref.at[0, x], ref.at[0, x], ref.at[0, (x - d) % 4], at_x(d)) for d in (1, 3, 2)]
        wait_all(along_x)
        then_z = [
            remote(ref.at[1, :, z], ref.at[1, :, z], ref.at[1, :, (z - d) % 4], at_z(d)) for d in (1, 3, 2)
        ]
        return then_x + then_z

    def matrix_one(ref):
        along_z = [
            remote(ref.at[x, z, c, 0], ref.at[x, z, c, 0], ref.at[x, (z - d) % 4, c, 0], at_z(d)) for d in (1, 3, 2)
        ]
        along_x = [
            remote(ref.at[x, z, c, 1], ref.at[x, z, c, 1], ref.at[(x - d) % 4, z, c, 1], at_x(d)) for d in (1, 3, 2)
        ]
        return along_z, along_x

    def matrix_pass(ref):
        return [remote(ref.at[x, z, c], ref.at[x, z, c], ref.at[x, z, o], sibling)]

    def matrix_two(ref, waits):
        along_z, along_x = waits
        passed = []
        wait_all(along_z)
        then_x = [
            remote(ref.at[x, :, c, 0], ref.at[x, :, c, 0], ref.at[(x - d) % 4, :, c, 0], at_x(d)) for d in (1, 3, 2)
        ]
        wait_all(along_x)
        then_z = [
            remote(ref.at[:, z, c, 1], ref.at[:, z, c, 1], ref.at[:, (z - d) % 4, c, 1], at_z(d)) for d in (1, 3, 2)
        ]
        for d in (1, 3, 2):
            k = (z - d) % 4
            passed.append(remote(ref.at[x, k, c, 0], ref.at[x, k, c, 0], ref.at[x, k, o, 0], sibling))
            k = (x - d) % 4
            passed.append(remote(ref.at[k, z, c, 1], ref.at[k, z, c, 1], ref.at[k, z, o, 1], sibling))
        return then_x, then_z, passed

    def matrix_end(ref, waits):
        then_x, then_z, passed = waits
        for n, d in enumerate((1, 3, 2)):
            k = (x - d) % 4
            then_x[n]()
            passed.append(remote(ref.at[k, :, c, 0], ref.at[k, :, c, 0], ref.at[k, :, o, 0], sibling))
            k = (z - d) % 4
            then_z[n]()
            passed.append(remote(ref.at[:, k, c, 1], ref.at[:, k, c, 1], ref.at[:, k, o, 1], sibling))
        return passed

    def hold(ref):
        for h in range(2):
            high, low = split(ref[h].reshape(1024, 128))
            op_high[:, 128 * h:128 * h + 128] = high
            op_low[:, 128 * h:128 * h + 128] = low

    wait_all(load_rhs)
    wait_all(swap_rhs0)
    rhs0_one = vector_one(rhs0)
    wait_all(load_inv0)
    inv0_pass = matrix_pass(inv0)
    inv0_one = matrix_one(inv0)
    rhs0_two = vector_two(rhs0, rhs0_one)
    inv0_two = matrix_two(inv0, inv0_one)
    wait_all(load_mid)
    mid_pass = matrix_pass(mid)
    wait_all(load_inv1)
    inv1_pass = matrix_pass(inv1)
    inv1_one = matrix_one(inv1)
    swap_panel0 = [remote(panel_anc.at[0, 0], panels.at[0, c], panels.at[0, o], sibling)]
    wait_all(swap_mask)
    wait_all(rhs0_two)
    hold(rhs0)
    inv0_end = matrix_end(inv0, inv0_two)
    inv1_two = matrix_two(inv1, inv1_one)
    wait_all(inv0_pass)
    wait_all(inv0_end)

    @pl.loop(0, 4)
    def _(i):
        got = product(split(inv0[i].reshape(256, 1024)), (op_high[...], op_low[...]))
        rows = pl.ds(pl.multiple_of(i * 256, 256), 256)
        first[rows] = got
        high, low = split(got)
        first_high[rows] = high
        first_low[rows] = low

    wait_all(load_rhs1)
    wait_all(swap_rhs1)
    wait_all(mid_pass)
    got = product(split(mid[x, z].reshape(64, 1024)), (first_high[...], first_low[...]))
    for h in range(2):
        tee[h, x, z] = rhs1[h] - got[:, 128 * h:128 * h + 128]
    tee_one = vector_one(tee)
    tee_two = vector_two(tee, tee_one)
    swap_panel1 = [remote(panel_anc.at[0, 1], panels.at[1, c], panels.at[1, o], sibling)]

    def masked(s):
        for core in range(2):
            for j in range(4):
                scale = mask_tile[core, s, j][0:1, 0:1]
                panels[s, core, 128 * j:128 * j + 128] = panels[s, core, 128 * j:128 * j + 128] * scale

    wait_all(load_panels)
    wait_all(swap_panel0)
    masked(0)

    @pl.loop(0, 4)
    def _(i):
        block = panels[0, i // 2, pl.ds(pl.multiple_of((i % 2) * 256, 256), 256)]
        update[i] = product(split(block), (first_high[...], first_low[...]))

    inv1_end = matrix_end(inv1, inv1_two)
    mid_one = matrix_one(mid)
    wait_all(swap_panel1)
    masked(1)
    wait_all(tee_two)
    hold(tee)
    wait_all(inv1_pass)
    wait_all(inv1_end)

    @pl.loop(0, 4)
    def _(i):
        got = product(split(inv1[i].reshape(256, 1024)), (op_high[...], op_low[...]))
        rows = pl.ds(pl.multiple_of(i * 256, 256), 256)
        second[rows] = got

    high, low = split(second[...])
    op_high[...] = high
    op_low[...] = low

    def update_block(i):
        block = panels[1, i // 2, pl.ds(pl.multiple_of((i % 2) * 256, 256), 256)]
        update[i] = update[i] + product(split(block), (op_high[...], op_low[...]))

    update_in = []
    for d in (1, 3, 2):
        k = (y + d) % 4
        update_block(k)
        update_in.append(remote(update.at[k], y_in.at[d - 1], y_in.at[d - 1], at_y(d)))
    update_block(y)
    mid_two = matrix_two(mid, mid_one)

    swap_anc = [
        remote(rhs_anc.at[:, other], anc_rhs.at[c], anc_rhs.at[o], sibling),
        remote(inv_anc, anc.at[c], anc.at[o], sibling),
    ]

    piece = x * 4 + z
    row = lax.broadcasted_iota(jnp.int32, (1024, 256), 0)
    inside = (row >= piece * 64) & (row < piece * 64 + 64)
    for s, solved in enumerate((first, second)):
        z_t[s] = jnp.where(inside, solved[...], 0.0).T

    wait_all(load_anc)
    wait_all(swap_anc[:1])
    wait_all(update_in)
    rows = pl.ds(pl.multiple_of((y % 2) * 256, 256), 256)
    value[y] = anc_rhs[y // 2, rows] - (update[y] + y_in[0] + y_in[1] + y_in[2])
    value_in = [remote(value.at[y], value.at[y], value.at[(y - d) % 4], at_y(d)) for d in (1, 3, 2)]
    mid_end = matrix_end(mid, mid_two)
    wait_all(swap_anc[1:])
    wait_all(mid_end)
    wait_all(value_in)
    high, low = split(value[...].reshape(1024, 256))
    op_high[...] = high
    op_low[...] = low

    @pl.loop(0, 4)
    def _(i):
        block = anc[i // 2, pl.ds(pl.multiple_of((i % 2) * 256, 256), 256)]
        got = product(split(block), (op_high[...], op_low[...]))
        fwd_t[:, pl.ds(pl.multiple_of(i * 256, 256), 256)] = got.T

    @pl.loop(0, 4)
    def _(n):
        cols = pl.ds(pl.multiple_of(n * 256, 256), 256)
        got = product(split(fwd_t[...]), split(anc[:, :, cols].reshape(1024, 256)))
        x_t[:, cols] = got
        x_out[n // 2, pl.ds(pl.multiple_of((n % 2) * 256, 256), 256)] = got.T

    done = [remote(x_out.at[o], x_anc.at[:, both], x_anc.at[:, other], sibling)]
    done.append(local(x_out.at[c], x_anc.at[:, both]))

    def reduce_one(s):
        along_x = [
            remote(w_send.at[s, 0, (x + d) % 4], r_first.at[s, 0, d - 1], r_first.at[s, 0, d - 1], at_x(d))
            for d in (1, 3, 2)
        ]
        along_z = [
            remote(w_send.at[s, 1, :, (z + d) % 4], r_first.at[s, 1, d - 1], r_first.at[s, 1, d - 1], at_z(d))
            for d in (1, 3, 2)
        ]
        return along_x, along_z

    def reduce_two(s, waits):
        along_x, along_z = waits
        wait_all(along_x)
        r_sum[s, 0] = (w_send[s, 0, x] + r_first[s, 0, 0]) + (r_first[s, 0, 1] + r_first[s, 0, 2])
        then_z = [
            remote(r_sum.at[s, 0, (z + d) % 4], r_second.at[s, 0, d - 1], r_second.at[s, 0, d - 1], at_z(d))
            for d in (1, 3, 2)
        ]
        wait_all(along_z)
        r_sum[s, 1] = (w_send[s, 1, :, z] + r_first[s, 1, 0]) + (r_first[s, 1, 1] + r_first[s, 1, 2])
        then_x = [
            remote(r_sum.at[s, 1, (x + d) % 4], r_second.at[s, 1, d - 1], r_second.at[s, 1, d - 1], at_x(d))
            for d in (1, 3, 2)
        ]
        return then_z + then_x

    def reduce_end(s, waits):
        wait_all(waits)
        for h, place in enumerate((z, x)):
            total = (r_sum[s, h, place] + r_second[s, h, 0]) + (r_second[s, h, 1] + r_second[s, h, 2])
            out_sub[s, :, 128 * h:128 * h + 128] = total
        out = remote(out_sub.at[s, theirs], x_sub.at[0, s, :, both], x_sub.at[0, s, :, other], sibling)
        return [out, local(out_sub.at[s, mine], x_sub.at[0, s, :, both])]

    def back(s, ref):
        @pl.loop(0, 4)
        def _(n):
            cols = pl.ds(pl.multiple_of(n * 256, 256), 256)
            got = product(split(z_t[s]), split(ref[:, :, :, :, :, cols].reshape(1024, 256)))
            if s == 1:
                w_t[:, cols] = got
            for h in range(2):
                w_send[s, h, n] = got[128 * h:128 * h + 128].T.reshape(4, 64, 128)

    @pl.loop(0, 4)
    def _(n):
        cols = pl.ds(pl.multiple_of(n * 256, 256), 256)
        z_t[1, :, cols] -= product(split(x_t[...]), split(panels[1, :, :, cols].reshape(1024, 256)))

    back(1, inv1)
    second_one = reduce_one(1)

    @pl.loop(0, 4)
    def _(n):
        cols = pl.ds(pl.multiple_of(n * 256, 256), 256)
        total = product(split(x_t[...]), split(panels[0, :, :, cols].reshape(1024, 256)))
        total += product(split(w_t[...]), split(mid[:, :, :, :, :, cols].reshape(1024, 256)))
        z_t[0, :, cols] -= total

    back(0, inv0)
    first_one = reduce_one(0)
    second_two = reduce_two(1, second_one)
    first_two = reduce_two(0, first_one)
    done += reduce_end(1, second_two)
    done += reduce_end(0, first_two)
    wait_all(done)
    for copy in sends:
        copy.wait_send()


def per_device(rhs_sub, rhs_anc, inv_sub, panel_mid, panel_anc, block_mask, inv_anc):
    any_space = pl.BlockSpec(memory_space=pl.ANY)
    vmem = pltpu.VMEM
    return pl.pallas_call(
        kernel,
        out_shape=(
            jax.ShapeDtypeStruct((1, 2, 32, 512), F32),
            jax.ShapeDtypeStruct((512, 512), F32),
        ),
        in_specs=[any_space] * 5 + [pl.BlockSpec(memory_space=pltpu.SMEM), any_space],
        out_specs=(any_space, any_space),
        scratch_shapes=[
            vmem((2, 4, 4, 64, 128), F32),
            vmem((2, 64, 128), F32),
            vmem((4, 4, 2, 2, 16, 1024), F32),
            vmem((4, 4, 2, 2, 16, 1024), F32),
            vmem((4, 4, 2, 2, 16, 1024), F32),
            vmem((2, 2, 512, 1024), F32),
            vmem((2, 512, 1024), F32),
            vmem((2, 512, 256), F32),
            vmem((2, 4, 4, 64, 128), F32),
            vmem((1024, 256), F32),
            vmem((1024, 256), F32),
            vmem((1024, 256), BF16),
            vmem((1024, 256), BF16),
            vmem((1024, 256), BF16),
            vmem((1024, 256), BF16),
            vmem((4, 256, 256), F32),
            vmem((3, 256, 256), F32),
            vmem((4, 256, 256), F32),
            vmem((256, 1024), F32),
            vmem((256, 1024), F32),
            vmem((2, 512, 256), F32),
            vmem((2, 256, 1024), F32),
            vmem((256, 1024), F32),
            vmem((2, 2, 4, 4, 64, 128), F32),
            vmem((2, 2, 3, 4, 64, 128), F32),
            vmem((2, 2, 4, 64, 128), F32),
            vmem((2, 2, 3, 64, 128), F32),
            vmem((2, 64, 256), F32),
            vmem((2, 2, 4, 8, 128), F32),
            pltpu.SemaphoreType.DMA((COPIES,)),
            pltpu.SemaphoreType.DMA((COPIES,)),
            pltpu.SemaphoreType.DMA((32,)),
        ],
        compiler_params=pltpu.CompilerParams(
            collective_id=0, has_side_effects=True, vmem_limit_bytes=60 * 2**20
        ),
        cost_estimate=pl.CostEstimate(flops=3 * 2 * 2900 * 2**20, bytes_accessed=10 * 2**20, transcendentals=0),
        name="solve",
    )(rhs_sub, rhs_anc, inv_sub, panel_mid, panel_anc, block_mask, inv_anc)


def solution(mesh):
    return jax.shard_map(
        per_device,
        mesh=mesh,
        in_specs=(
            P("leaf", None, "row", None),
            P("row", None),
            P("leaf", None, "row", None),
            P("leaf", "row", None),
            P("leaf", None, "row", None),
            P("leaf", None, "row"),
            P("row", None),
        ),
        out_specs=(P("leaf", None, "row", None), P("row", None)),
        check_vma=False,
    )
```

```python
import functools

import jax
import jax.numpy as jnp
from jax import lax
from jax.experimental import pallas as pl
from jax.experimental.pallas import tpu as pltpu
from jax.sharding import PartitionSpec as P

F32 = jnp.float32
BF16 = jnp.bfloat16
MESH = pl.DeviceIdType.MESH
COPIES = 256


def split(value):
    high = value.astype(BF16)
    return high, (value - high.astype(F32)).astype(BF16)


def dot(left, right):
    return jnp.dot(left, right, preferred_element_type=F32)


def product(left, right):
    left_high, left_low = left
    right_high, right_low = right
    return dot(left_high, right_high) + (dot(left_high, right_low) + dot(left_low, right_high))


def product_t(left, right):
    def one(a, b):
        return lax.dot_general(a, b, (((0,), (0,)), ((), ())), preferred_element_type=F32)

    left_high, left_low = left
    right_high, right_low = right
    return one(left_high, right_high) + (one(left_high, right_low) + one(left_low, right_high))


def kernel(
    rhs_sub, rhs_anc, inv_sub, panel_mid, panel_anc, mask, inv_anc,
    x_sub, x_anc,
    rhs0, rhs1, inv0, inv1, mid, panels, anc, anc_rhs,
    first, tee, op_high, op_low, first_high, first_low,
    q_high, q_low, g_high, g_low,
    update, y_in, value, x_out, own,
    w_part, w_send, r_first, r_sum, r_second, out_sub, mask_tile,
    send_sem, recv_sem, local_sem,
):
    y = lax.axis_index("leaf")
    r = lax.axis_index("row")
    x, z, c = r // 8, (r // 2) % 4, r % 2
    o = 1 - c

    def at_x(d):
        return (y, ((x + d) % 4) * 8 + z * 2 + c)

    def at_z(d):
        return (y, x * 8 + ((z + d) % 4) * 2 + c)

    def at_y(d):
        return ((y + d) % 4, r)

    sibling = (y, x * 8 + z * 2 + o)
    ring = (1, 3, 2)

    count = [0, 0]
    sends = []

    def remote(src, dst, landing, device):
        index = count[0]
        count[0] += 1
        out = pltpu.make_async_remote_copy(
            src_ref=src, dst_ref=dst, send_sem=send_sem.at[index], recv_sem=recv_sem.at[index],
            device_id=device, device_id_type=MESH,
        )
        out.start()
        sends.append(out)
        into = pltpu.make_async_remote_copy(
            src_ref=landing, dst_ref=landing, send_sem=send_sem.at[index], recv_sem=recv_sem.at[index],
            device_id=device, device_id_type=MESH,
        )
        return into.wait_recv

    def local(src, dst):
        index = count[1]
        count[1] += 1
        copy = pltpu.make_async_copy(src, dst, local_sem.at[index])
        copy.start()
        return copy.wait

    def wait_all(waits):
        for wait in waits:
            wait()

    def columns(core, half):
        return pl.ds(pl.multiple_of(core * 256 + half * 128, 128), 128)

    def block(i):
        return pl.ds(pl.multiple_of(i * 256, 256), 256)

    mine = pl.ds(pl.multiple_of(c * 32, 32), 32)
    theirs = pl.ds(pl.multiple_of(o * 32, 32), 32)
    both = block(c)
    other = block(o)

    load_rhs0 = [local(rhs_sub.at[0, 0, :, columns(c, h)], rhs0.at[h, x, z, mine]) for h in range(2)]
    load_inv0 = [local(inv_sub.at[0, 0, pl.ds(16 * h, 16)], inv0.at[x, z, c, h]) for h in range(2)]
    load_rhs1 = [local(rhs_sub.at[0, 1, :, columns(c, h)], rhs1.at[h, mine]) for h in range(2)]
    load_inv1 = [local(inv_sub.at[0, 1, pl.ds(16 * h, 16)], inv1.at[x, z, c, h]) for h in range(2)]
    load_mid = [local(panel_mid.at[0, pl.ds(16 * h, 16)], mid.at[x, z, c, h]) for h in range(2)]
    for s in range(2):
        for j in range(4):
            mask_tile[c, s, j] = jnp.full((8, 128), mask[0, s, j].astype(F32), F32)

    barrier = pltpu.get_barrier_semaphore()
    for device in [at_x(1), at_x(2), at_x(3), at_z(1), at_z(2), at_z(3), at_y(1), at_y(2), at_y(3), sibling]:
        pl.semaphore_signal(barrier, inc=1, device_id=device, device_id_type=MESH)
    pl.semaphore_wait(barrier, 10)

    swap_rhs0 = [
        remote(rhs_sub.at[0, 0, :, columns(o, h)], rhs0.at[h, x, z, mine], rhs0.at[h, x, z, theirs], sibling)
        for h in range(2)
    ]

    def vector_start(ref):
        near, far = [[], []], [[], []]
        for d in ring:
            near[0].append(remote(ref.at[0, x, z], ref.at[0, x, z], ref.at[0, x, (z - d) % 4], at_z(d)))
            near[1].append(remote(ref.at[1, x, z], ref.at[1, x, z], ref.at[1, (x - d) % 4, z], at_x(d)))
        for d in ring:
            far[0].append(remote(ref.at[0, x, z], ref.at[0, x, z], ref.at[0, (x - d) % 4, z], at_x(d)))
            far[1].append(remote(ref.at[1, x, z], ref.at[1, x, z], ref.at[1, x, (z - d) % 4], at_z(d)))
        return near, far

    def vector_pass(ref, waits):
        near, far = waits
        for n, e in enumerate(ring):
            k = (z - e) % 4
            near[0][n]()
            for d in ring:
                far[0].append(remote(ref.at[0, x, k], ref.at[0, x, k], ref.at[0, (x - d) % 4, k], at_x(d)))
            k = (x - e) % 4
            near[1][n]()
            for d in ring:
                far[1].append(remote(ref.at[1, k, z], ref.at[1, k, z], ref.at[1, k, (z - d) % 4], at_z(d)))
        return far

    def vector_end(ref, far, high_ref, low_ref):
        for h in range(2):
            wait_all(far[h])
            high, low = split(ref[h].reshape(1024, 128))
            high_ref[:, 128 * h:128 * h + 128] = high
            low_ref[:, 128 * h:128 * h + 128] = low

    def matrix_share(ref):
        return [remote(ref.at[x, z, c], ref.at[x, z, c], ref.at[x, z, o], sibling)]

    def matrix_start(ref):
        near = [[], []]
        for d in ring:
            near[0].append(remote(ref.at[x, z, c, 0], ref.at[x, z, c, 0], ref.at[x, (z - d) % 4, c, 0], at_z(d)))
            near[1].append(remote(ref.at[x, z, c, 1], ref.at[x, z, c, 1], ref.at[(x - d) % 4, z, c, 1], at_x(d)))
        return near

    def matrix_near(ref, near):
        shared = []
        for n, d in enumerate(ring):
            near[0][n]()
            near[1][n]()
            k = (z - d) % 4
            shared.append(remote(ref.at[x, k, c, 0], ref.at[x, k, c, 0], ref.at[x, k, o, 0], sibling))
            k = (x - d) % 4
            shared.append(remote(ref.at[k, z, c, 1], ref.at[k, z, c, 1], ref.at[k, z, o, 1], sibling))
        return shared

    def matrix_far(ref, distances):
        far = []
        for d in distances:
            k = (x - d) % 4
            far.append((d, 0, remote(ref.at[x, :, c, 0], ref.at[x, :, c, 0], ref.at[k, :, c, 0], at_x(d))))
            k = (z - d) % 4
            far.append((d, 1, remote(ref.at[:, z, c, 1], ref.at[:, z, c, 1], ref.at[:, k, c, 1], at_z(d))))
        return far

    def matrix_end(ref, far):
        shared = []
        for d, h, wait in far:
            wait()
            if h == 0:
                k = (x - d) % 4
                shared.append(remote(ref.at[k, :, c, 0], ref.at[k, :, c, 0], ref.at[k, :, o, 0], sibling))
            else:
                k = (z - d) % 4
                shared.append(remote(ref.at[:, k, c, 1], ref.at[:, k, c, 1], ref.at[:, k, o, 1], sibling))
        return shared

    def masked(s):
        for core in range(2):
            for j in range(4):
                scale = mask_tile[core, s, j][0:1, 0:1]
                panels[s, core, 128 * j:128 * j + 128] = panels[s, core, 128 * j:128 * j + 128] * scale

    def panel(s):
        return panels[s].reshape(1024, 1024)

    def whole(ref):
        return ref[...].reshape(1024, 1024)

    def chip_rows(ref):
        return split(ref[x, z].reshape(64, 1024))

    wait_all(load_rhs0)
    wait_all(swap_rhs0)
    gather0 = vector_start(rhs0)
    wait_all(load_inv0)
    share_inv0 = matrix_share(inv0)
    swap_rhs1 = [
        remote(rhs_sub.at[0, 1, :, columns(o, h)], rhs1.at[h, mine], rhs1.at[h, theirs], sibling)
        for h in range(2)
    ]
    swap_mask = [remote(mask_tile.at[c], mask_tile.at[c], mask_tile.at[o], sibling)]
    wait_all(load_mid)
    share_mid = matrix_share(mid)
    wait_all(load_inv1)
    share_inv1 = matrix_share(inv1)
    gather0 = vector_pass(rhs0, gather0)
    near_inv1 = matrix_start(inv1)
    load_panels = [local(panel_anc.at[0, s], panels.at[s, c]) for s in (1, 0)]
    swap_panels = [remote(panel_anc.at[0, s], panels.at[s, c], panels.at[s, o], sibling) for s in (1, 0)]
    load_anc = [local(rhs_anc.at[:, both], anc_rhs.at[c]), local(inv_anc, anc.at[c])]
    swap_anc = [
        remote(rhs_anc.at[:, other], anc_rhs.at[c], anc_rhs.at[o], sibling),
        remote(inv_anc, anc.at[c], anc.at[o], sibling),
    ]
    wait_all(share_inv0)
    vector_end(rhs0, gather0, op_high, op_low)
    got = product(chip_rows(inv0), (op_high[...], op_low[...]))
    own[0] = got
    for h in range(2):
        first[h, x, z] = got[:, 128 * h:128 * h + 128]
    gather1 = vector_start(first)
    share_inv1 += matrix_near(inv1, near_inv1)
    gather1 = vector_pass(first, gather1)
    far_inv1 = matrix_far(inv1, (1, 3))
    wait_all(swap_mask)
    wait_all(load_panels)
    wait_all(swap_panels)
    masked(1)
    masked(0)
    wait_all(load_rhs1)
    wait_all(swap_rhs1)
    wait_all(share_mid)
    vector_end(first, gather1, first_high, first_low)
    got = product(chip_rows(mid), (first_high[...], first_low[...]))
    for h in range(2):
        tee[h, x, z] = rhs1[h] - got[:, 128 * h:128 * h + 128]
    gather2 = vector_start(tee)
    far_inv1 += matrix_far(inv1, (2,))
    gather2 = vector_pass(tee, gather2)
    update[...] = product(split(panel(0)), (first_high[...], first_low[...])).reshape(4, 256, 256)
    share_inv1 += matrix_end(inv1, far_inv1)
    wait_all(share_inv1)
    near_inv0 = matrix_start(inv0)
    near_mid = matrix_start(mid)
    for n in range(4):
        cols = slice(256 * n, 256 * n + 256)
        below = inv1[n:, :, :, :, :, cols].reshape(1024 - 256 * n, 256)
        left = panels[1, :, :, 256 * n:].reshape(1024, 1024 - 256 * n)
        high, low = split(product(split(left), split(below)))
        q_high[:, cols] = high
        q_low[:, cols] = low
    vector_end(tee, gather2, op_high, op_low)

    def update_block(i):
        rows = block(i)
        update[i] = update[i] + product((q_high[rows], q_low[rows]), (op_high[...], op_low[...]))

    update_in = []
    for d in ring:
        k = (y + d) % 4
        update_block(k)
        update_in.append(remote(update.at[k], y_in.at[d - 1], y_in.at[d - 1], at_y(d)))
    update_block(y)
    share_inv0 = matrix_near(inv0, near_inv0)
    far_inv0 = matrix_far(inv0, ring)
    share_mid = matrix_near(mid, near_mid)
    far_mid = matrix_far(mid, ring)
    own[1] = product(chip_rows(inv1), (op_high[...], op_low[...]))
    for s, ref in enumerate((inv0, inv1)):
        w_part[s] = product_t(chip_rows(ref), split(own[s]))
    wait_all(load_anc)
    wait_all(swap_anc)
    for n in range(4):
        cols = slice(256 * n, 256 * n + 256)
        high, low = split(product_t(split(whole(anc)), split(anc[:, :, cols].reshape(1024, 256))))
        g_high[:, cols] = high
        g_low[:, cols] = low
    wait_all(update_in)
    rows = block(y % 2)
    value[y] = anc_rhs[y // 2, rows] - ((update[y] + y_in[0]) + (y_in[1] + y_in[2]))
    value_in = [remote(value.at[y], value.at[y], value.at[(y - d) % 4], at_y(d)) for d in ring]
    share_inv0 += matrix_end(inv0, far_inv0)

    def solve_part(i):
        cols = block(i)
        return product((g_high[:, cols], g_low[:, cols]), split(value[i])).reshape(2, 512, 256)

    x_out[...] = solve_part(y)
    share_mid += matrix_end(mid, far_mid)
    for n, d in enumerate(ring):
        value_in[n]()
        x_out[...] += solve_part((y - d) % 4)
    high, low = split(x_out[...].reshape(1024, 256))
    op_high[...] = high
    op_low[...] = low

    def reduce_start(s):
        landed = {}
        for e in (2, 1, 3, 0):
            k = (z + e) % 4
            landed[0, e] = [
                remote(w_send.at[s, 0, (x + d) % 4, k], r_first.at[s, 0, d - 1, k], r_first.at[s, 0, d - 1, k], at_x(d))
                for d in ring
            ]
            k = (x + e) % 4
            landed[1, e] = [
                remote(w_send.at[s, 1, k, (z + d) % 4], r_first.at[s, 1, d - 1, k], r_first.at[s, 1, d - 1, k], at_z(d))
                for d in ring
            ]
        return landed

    def reduce_sum(s, landed, h, e):
        wait_all(landed[h, e])
        k = ((z if h == 0 else x) + e) % 4
        kept = w_send[s, 0, x, k] if h == 0 else w_send[s, 1, k, z]
        return (kept + r_first[s, h, 0, k]) + (r_first[s, h, 1, k] + r_first[s, h, 2, k])

    def reduce_pass(s, landed):
        waits = [[], []]
        for e in (2, 1, 3):
            for h in range(2):
                r_sum[s, h, e - 1] = reduce_sum(s, landed, h, e)
                device = at_z(e) if h == 0 else at_x(e)
                waits[h].append(
                    remote(r_sum.at[s, h, e - 1], r_second.at[s, h, e - 1], r_second.at[s, h, e - 1], device)
                )
        return waits

    def reduce_end(s, landed, waits):
        for h in range(2):
            total = reduce_sum(s, landed, h, 0)
            wait_all(waits[h])
            total += r_second[s, h, 0] + (r_second[s, h, 1] + r_second[s, h, 2])
            out_sub[s, :, 128 * h:128 * h + 128] = total
        out = remote(out_sub.at[s, theirs], x_sub.at[0, s, :, both], x_sub.at[0, s, :, other], sibling)
        return [out, local(out_sub.at[s, mine], x_sub.at[0, s, :, both])]

    def put(s, total):
        for h in range(2):
            w_send[s, h] = total[:, 128 * h:128 * h + 128].reshape(4, 4, 64, 128)

    total = w_part[1] - product_t((q_high[...], q_low[...]), (op_high[...], op_low[...]))
    put(1, total)
    landed1 = reduce_start(1)
    high, low = split(total)
    first_high[...] = high
    first_low[...] = low
    done = [remote(x_out.at[o], x_anc.at[:, both], x_anc.at[:, other], sibling)]
    done.append(local(x_out.at[c], x_anc.at[:, both]))
    total = product_t(split(panel(0)), (op_high[...], op_low[...]))
    wait_all(share_mid)
    total += product_t(split(whole(mid)), (first_high[...], first_low[...]))
    high, low = split(total)
    op_high[...] = high
    op_low[...] = low
    wait_all(share_inv0)
    put(0, w_part[0] - product_t(split(whole(inv0)), (op_high[...], op_low[...])))
    landed0 = reduce_start(0)
    waits1 = reduce_pass(1, landed1)
    done += reduce_end(1, landed1, waits1)
    waits0 = reduce_pass(0, landed0)
    done += reduce_end(0, landed0, waits0)
    wait_all(done)
    for copy in sends:
        copy.wait_send()


def per_device(rhs_sub, rhs_anc, inv_sub, panel_mid, panel_anc, block_mask, inv_anc):
    any_space = pl.BlockSpec(memory_space=pl.ANY)
    vmem = pltpu.VMEM
    return pl.pallas_call(
        kernel,
        out_shape=(
            jax.ShapeDtypeStruct((1, 2, 32, 512), F32),
            jax.ShapeDtypeStruct((512, 512), F32),
        ),
        in_specs=[any_space] * 5 + [pl.BlockSpec(memory_space=pltpu.SMEM), any_space],
        out_specs=(any_space, any_space),
        scratch_shapes=[
            vmem((2, 4, 4, 64, 128), F32),
            vmem((2, 64, 128), F32),
            vmem((4, 4, 2, 2, 16, 1024), F32),
            vmem((4, 4, 2, 2, 16, 1024), F32),
            vmem((4, 4, 2, 2, 16, 1024), F32),
            vmem((2, 2, 512, 1024), F32),
            vmem((2, 512, 1024), F32),
            vmem((2, 512, 256), F32),
            vmem((2, 4, 4, 64, 128), F32),
            vmem((2, 4, 4, 64, 128), F32),
            vmem((1024, 256), BF16),
            vmem((1024, 256), BF16),
            vmem((1024, 256), BF16),
            vmem((1024, 256), BF16),
            vmem((1024, 1024), BF16),
            vmem((1024, 1024), BF16),
            vmem((1024, 1024), BF16),
            vmem((1024, 1024), BF16),
            vmem((4, 256, 256), F32),
            vmem((3, 256, 256), F32),
            vmem((4, 256, 256), F32),
            vmem((2, 512, 256), F32),
            vmem((2, 64, 256), F32),
            vmem((2, 1024, 256), F32),
            vmem((2, 2, 4, 4, 64, 128), F32),
            vmem((2, 2, 3, 4, 64, 128), F32),
            vmem((2, 2, 3, 64, 128), F32),
            vmem((2, 2, 3, 64, 128), F32),
            vmem((2, 64, 256), F32),
            vmem((2, 2, 4, 8, 128), F32),
            pltpu.SemaphoreType.DMA((COPIES,)),
            pltpu.SemaphoreType.DMA((COPIES,)),
            pltpu.SemaphoreType.DMA((32,)),
        ],
        compiler_params=pltpu.CompilerParams(
            collective_id=0, has_side_effects=True, vmem_limit_bytes=60 * 2**20
        ),
        cost_estimate=pl.CostEstimate(flops=3 * 2 * 2900 * 2**20, bytes_accessed=10 * 2**20, transcendentals=0),
        name="solve",
    )(rhs_sub, rhs_anc, inv_sub, panel_mid, panel_anc, block_mask, inv_anc)


def solution(mesh):
    return jax.shard_map(
        per_device,
        mesh=mesh,
        in_specs=(
            P("leaf", None, "row", None),
            P("row", None),
            P("leaf", None, "row", None),
            P("leaf", "row", None),
            P("leaf", None, "row", None),
            P("leaf", None, "row"),
            P("row", None),
        ),
        out_specs=(P("leaf", None, "row", None), P("row", None)),
        check_vma=False,
    )
```

```python
import functools

import jax
import jax.numpy as jnp
from jax import lax
from jax.experimental import pallas as pl
from jax.experimental.pallas import tpu as pltpu
from jax.sharding import PartitionSpec as P

F32 = jnp.float32
BF16 = jnp.bfloat16
MESH = pl.DeviceIdType.MESH
COPIES = 256


def split(value):
    high = value.astype(BF16)
    return high, (value - high.astype(F32)).astype(BF16)


def dot(left, right):
    return jnp.dot(left, right, preferred_element_type=F32)


def product(left, right):
    left_high, left_low = left
    right_high, right_low = right
    return dot(left_high, right_high) + (dot(left_high, right_low) + dot(left_low, right_high))


def product_t(left, right):
    def one(a, b):
        return lax.dot_general(a, b, (((0,), (0,)), ((), ())), preferred_element_type=F32)

    left_high, left_low = left
    right_high, right_low = right
    return one(left_high, right_high) + (one(left_high, right_low) + one(left_low, right_high))


def kernel(
    rhs_sub, rhs_anc, inv_sub, panel_mid, panel_anc, mask, inv_anc,
    x_sub, x_anc,
    rhs0, rhs1, inv0, inv1, mid, panels, anc, anc_rhs,
    first, tee, op_high, op_low, first_high, first_low,
    q_high, q_low, g_high, g_low,
    update, y_in, value, x_out, own,
    w_part, w_send, r_first, r_sum, r_second, out_sub, mask_tile,
    send_sem, recv_sem, local_sem,
):
    y = lax.axis_index("leaf")
    r = lax.axis_index("row")
    x, z, c = r // 8, (r // 2) % 4, r % 2
    o = 1 - c

    def at_x(d):
        return (y, ((x + d) % 4) * 8 + z * 2 + c)

    def at_z(d):
        return (y, x * 8 + ((z + d) % 4) * 2 + c)

    def at_y(d):
        return ((y + d) % 4, r)

    sibling = (y, x * 8 + z * 2 + o)
    ring = (1, 3, 2)

    count = [0, 0]
    sends = []

    def remote(src, dst, landing, device):
        index = count[0]
        count[0] += 1
        out = pltpu.make_async_remote_copy(
            src_ref=src, dst_ref=dst, send_sem=send_sem.at[index], recv_sem=recv_sem.at[index],
            device_id=device, device_id_type=MESH,
        )
        out.start()
        sends.append(out)
        into = pltpu.make_async_remote_copy(
            src_ref=landing, dst_ref=landing, send_sem=send_sem.at[index], recv_sem=recv_sem.at[index],
            device_id=device, device_id_type=MESH,
        )
        return into.wait_recv

    def local(src, dst):
        index = count[1]
        count[1] += 1
        copy = pltpu.make_async_copy(src, dst, local_sem.at[index])
        copy.start()
        return copy.wait

    def wait_all(waits):
        for wait in waits:
            wait()

    def columns(core, half):
        return pl.ds(pl.multiple_of(core * 256 + half * 128, 128), 128)

    def block(i):
        return pl.ds(pl.multiple_of(i * 256, 256), 256)

    mine = pl.ds(pl.multiple_of(c * 32, 32), 32)
    theirs = pl.ds(pl.multiple_of(o * 32, 32), 32)
    both = block(c)
    other = block(o)

    load_rhs0 = [local(rhs_sub.at[0, 0, :, columns(c, h)], rhs0.at[h, x, z, mine]) for h in range(2)]
    load_inv0 = [local(inv_sub.at[0, 0, pl.ds(16 * h, 16)], inv0.at[x, z, c, h]) for h in range(2)]
    load_rhs1 = [local(rhs_sub.at[0, 1, :, columns(c, h)], rhs1.at[h, mine]) for h in range(2)]
    load_inv1 = [local(inv_sub.at[0, 1, pl.ds(16 * h, 16)], inv1.at[x, z, c, h]) for h in range(2)]
    load_mid = [local(panel_mid.at[0, pl.ds(16 * h, 16)], mid.at[x, z, c, h]) for h in range(2)]
    for s in range(2):
        for j in range(4):
            mask_tile[c, s, j] = jnp.full((8, 128), mask[0, s, j].astype(F32), F32)

    barrier = pltpu.get_barrier_semaphore()
    for device in [at_x(1), at_x(2), at_x(3), at_z(1), at_z(2), at_z(3), at_y(1), at_y(2), at_y(3), sibling]:
        pl.semaphore_signal(barrier, inc=1, device_id=device, device_id_type=MESH)
    pl.semaphore_wait(barrier, 10)

    swap_rhs0 = [
        remote(rhs_sub.at[0, 0, :, columns(o, h)], rhs0.at[h, x, z, mine], rhs0.at[h, x, z, theirs], sibling)
        for h in range(2)
    ]

    def vector_start(ref):
        near, far = [[], []], [[], []]
        for d in ring:
            near[0].append(remote(ref.at[0, x, z], ref.at[0, x, z], ref.at[0, x, (z - d) % 4], at_z(d)))
            near[1].append(remote(ref.at[1, x, z], ref.at[1, x, z], ref.at[1, (x - d) % 4, z], at_x(d)))
        for d in ring:
            far[0].append(remote(ref.at[0, x, z], ref.at[0, x, z], ref.at[0, (x - d) % 4, z], at_x(d)))
            far[1].append(remote(ref.at[1, x, z], ref.at[1, x, z], ref.at[1, x, (z - d) % 4], at_z(d)))
        return near, far

    def vector_pass(ref, waits):
        near, far = waits
        for n, e in enumerate(ring):
            k = (z - e) % 4
            near[0][n]()
            for d in ring:
                far[0].append(remote(ref.at[0, x, k], ref.at[0, x, k], ref.at[0, (x - d) % 4, k], at_x(d)))
            k = (x - e) % 4
            near[1][n]()
            for d in ring:
                far[1].append(remote(ref.at[1, k, z], ref.at[1, k, z], ref.at[1, k, (z - d) % 4], at_z(d)))
        return far

    def vector_end(ref, far, high_ref, low_ref):
        for h in range(2):
            wait_all(far[h])
            high, low = split(ref[h].reshape(1024, 128))
            high_ref[:, 128 * h:128 * h + 128] = high
            low_ref[:, 128 * h:128 * h + 128] = low

    def matrix_share(ref):
        return [remote(ref.at[x, z, c], ref.at[x, z, c], ref.at[x, z, o], sibling)]

    def matrix_start(ref):
        near = [[], []]
        for d in ring:
            near[0].append(remote(ref.at[x, z, c, 0], ref.at[x, z, c, 0], ref.at[x, (z - d) % 4, c, 0], at_z(d)))
            near[1].append(remote(ref.at[x, z, c, 1], ref.at[x, z, c, 1], ref.at[(x - d) % 4, z, c, 1], at_x(d)))
        return near

    def matrix_near(ref, near):
        shared = []
        for n, d in enumerate(ring):
            near[0][n]()
            near[1][n]()
            k = (z - d) % 4
            shared.append(remote(ref.at[x, k, c, 0], ref.at[x, k, c, 0], ref.at[x, k, o, 0], sibling))
            k = (x - d) % 4
            shared.append(remote(ref.at[k, z, c, 1], ref.at[k, z, c, 1], ref.at[k, z, o, 1], sibling))
        return shared

    def matrix_far(ref, distances):
        far = []
        for d in distances:
            k = (x - d) % 4
            far.append((d, 0, remote(ref.at[x, :, c, 0], ref.at[x, :, c, 0], ref.at[k, :, c, 0], at_x(d))))
            k = (z - d) % 4
            far.append((d, 1, remote(ref.at[:, z, c, 1], ref.at[:, z, c, 1], ref.at[:, k, c, 1], at_z(d))))
        return far

    def matrix_end(ref, far):
        shared = []
        for d, h, wait in far:
            wait()
            if h == 0:
                k = (x - d) % 4
                shared.append(remote(ref.at[k, :, c, 0], ref.at[k, :, c, 0], ref.at[k, :, o, 0], sibling))
            else:
                k = (z - d) % 4
                shared.append(remote(ref.at[:, k, c, 1], ref.at[:, k, c, 1], ref.at[:, k, o, 1], sibling))
        return shared

    def masked(s):
        for core in range(2):
            for j in range(4):
                scale = mask_tile[core, s, j][0:1, 0:1]
                panels[s, core, 128 * j:128 * j + 128] = panels[s, core, 128 * j:128 * j + 128] * scale

    def panel(s):
        return panels[s].reshape(1024, 1024)

    def whole(ref):
        return ref[...].reshape(1024, 1024)

    def chip_rows(ref):
        return split(ref[x, z].reshape(64, 1024))

    wait_all(load_rhs0)
    wait_all(swap_rhs0)
    gather0 = vector_start(rhs0)
    wait_all(load_inv0)
    share_inv0 = matrix_share(inv0)
    swap_rhs1 = [
        remote(rhs_sub.at[0, 1, :, columns(o, h)], rhs1.at[h, mine], rhs1.at[h, theirs], sibling)
        for h in range(2)
    ]
    swap_mask = [remote(mask_tile.at[c], mask_tile.at[c], mask_tile.at[o], sibling)]
    wait_all(load_mid)
    share_mid = matrix_share(mid)
    wait_all(load_inv1)
    share_inv1 = matrix_share(inv1)
    gather0 = vector_pass(rhs0, gather0)
    near_inv1 = matrix_start(inv1)
    load_anc = [local(inv_anc, anc.at[c])]
    swap_anc = [remote(inv_anc, anc.at[c], anc.at[o], sibling)]
    load_panels = [local(panel_anc.at[0, s], panels.at[s, c]) for s in range(2)]
    swap_panels = [remote(panel_anc.at[0, s], panels.at[s, c], panels.at[s, o], sibling) for s in range(2)]
    load_anc_rhs = [local(rhs_anc.at[:, both], anc_rhs.at[c])]
    swap_anc_rhs = [remote(rhs_anc.at[:, other], anc_rhs.at[c], anc_rhs.at[o], sibling)]
    wait_all(share_inv0)
    vector_end(rhs0, gather0, op_high, op_low)
    got = product(chip_rows(inv0), (op_high[...], op_low[...]))
    own[0] = got
    for h in range(2):
        first[h, x, z] = got[:, 128 * h:128 * h + 128]
    gather1 = vector_start(first)
    share_inv1 += matrix_near(inv1, near_inv1)
    gather1 = vector_pass(first, gather1)
    far_inv1 = matrix_far(inv1, (1, 3))
    wait_all(load_anc)
    wait_all(swap_anc)
    for n in range(4):
        cols = slice(256 * n, 256 * n + 256)
        high, low = split(product_t(split(whole(anc)), split(anc[:, :, cols].reshape(1024, 256))))
        g_high[:, cols] = high
        g_low[:, cols] = low
    wait_all(load_rhs1)
    wait_all(swap_rhs1)
    wait_all(share_mid)
    vector_end(first, gather1, first_high, first_low)
    got = product(chip_rows(mid), (first_high[...], first_low[...]))
    for h in range(2):
        tee[h, x, z] = rhs1[h] - got[:, 128 * h:128 * h + 128]
    gather2 = vector_start(tee)
    far_inv1 += matrix_far(inv1, (2,))
    gather2 = vector_pass(tee, gather2)
    near_inv0 = matrix_start(inv0)
    wait_all(swap_mask)
    wait_all(load_panels)
    wait_all(swap_panels)
    masked(0)
    update[...] = product(split(panel(0)), (first_high[...], first_low[...])).reshape(4, 256, 256)
    masked(1)
    share_inv1 += matrix_end(inv1, far_inv1)
    wait_all(share_inv1)
    near_mid = matrix_start(mid)
    for n in range(4):
        cols = slice(256 * n, 256 * n + 256)
        below = inv1[n:, :, :, :, :, cols].reshape(1024 - 256 * n, 256)
        left = panels[1, :, :, 256 * n:].reshape(1024, 1024 - 256 * n)
        high, low = split(product(split(left), split(below)))
        q_high[:, cols] = high
        q_low[:, cols] = low
    share_inv0 = matrix_near(inv0, near_inv0)
    far_inv0 = matrix_far(inv0, ring)
    vector_end(tee, gather2, op_high, op_low)

    def update_block(i):
        rows = block(i)
        update[i] = update[i] + product((q_high[rows], q_low[rows]), (op_high[...], op_low[...]))

    update_in = []
    for d in ring:
        k = (y + d) % 4
        update_block(k)
        update_in.append(remote(update.at[k], y_in.at[d - 1], y_in.at[d - 1], at_y(d)))
    update_block(y)
    share_mid = matrix_near(mid, near_mid)
    far_mid = matrix_far(mid, ring)
    own[1] = product(chip_rows(inv1), (op_high[...], op_low[...]))
    for s, ref in enumerate((inv0, inv1)):
        w_part[s] = product_t(chip_rows(ref), split(own[s]))
    wait_all(load_anc_rhs)
    wait_all(swap_anc_rhs)
    wait_all(update_in)
    rows = block(y % 2)
    value[y] = anc_rhs[y // 2, rows] - ((update[y] + y_in[0]) + (y_in[1] + y_in[2]))
    value_in = [remote(value.at[y], value.at[y], value.at[(y - d) % 4], at_y(d)) for d in ring]
    share_inv0 += matrix_end(inv0, far_inv0)

    def solve_part(i):
        cols = block(i)
        return product((g_high[:, cols], g_low[:, cols]), split(value[i])).reshape(2, 512, 256)

    x_out[...] = solve_part(y)
    for n, d in enumerate(ring):
        value_in[n]()
        x_out[...] += solve_part((y - d) % 4)
    high, low = split(x_out[...].reshape(1024, 256))
    op_high[...] = high
    op_low[...] = low

    def reduce_start(s):
        landed = {}
        for e in (2, 1, 3, 0):
            k = (z + e) % 4
            landed[0, e] = [
                remote(w_send.at[s, 0, (x + d) % 4, k], r_first.at[s, 0, d - 1, k], r_first.at[s, 0, d - 1, k], at_x(d))
                for d in ring
            ]
            k = (x + e) % 4
            landed[1, e] = [
                remote(w_send.at[s, 1, k, (z + d) % 4], r_first.at[s, 1, d - 1, k], r_first.at[s, 1, d - 1, k], at_z(d))
                for d in ring
            ]
        return landed

    def reduce_sum(s, landed, h, e):
        wait_all(landed[h, e])
        k = ((z if h == 0 else x) + e) % 4
        kept = w_send[s, 0, x, k] if h == 0 else w_send[s, 1, k, z]
        return (kept + r_first[s, h, 0, k]) + (r_first[s, h, 1, k] + r_first[s, h, 2, k])

    def reduce_pass(s, landed):
        waits = [[], []]
        for e in (2, 1, 3):
            for h in range(2):
                r_sum[s, h, e - 1] = reduce_sum(s, landed, h, e)
                device = at_z(e) if h == 0 else at_x(e)
                waits[h].append(
                    remote(r_sum.at[s, h, e - 1], r_second.at[s, h, e - 1], r_second.at[s, h, e - 1], device)
                )
        return waits

    def reduce_end(s, landed, waits):
        for h in range(2):
            total = reduce_sum(s, landed, h, 0)
            wait_all(waits[h])
            total += r_second[s, h, 0] + (r_second[s, h, 1] + r_second[s, h, 2])
            out_sub[s, :, 128 * h:128 * h + 128] = total
        out = remote(out_sub.at[s, theirs], x_sub.at[0, s, :, both], x_sub.at[0, s, :, other], sibling)
        return [out, local(out_sub.at[s, mine], x_sub.at[0, s, :, both])]

    def put(s, total):
        for h in range(2):
            w_send[s, h] = total[:, 128 * h:128 * h + 128].reshape(4, 4, 64, 128)

    total = w_part[1] - product_t((q_high[...], q_low[...]), (op_high[...], op_low[...]))
    put(1, total)
    landed1 = reduce_start(1)
    share_mid += matrix_end(mid, far_mid)
    high, low = split(total)
    first_high[...] = high
    first_low[...] = low
    done = [remote(x_out.at[o], x_anc.at[:, both], x_anc.at[:, other], sibling)]
    done.append(local(x_out.at[c], x_anc.at[:, both]))
    total = product_t(split(panel(0)), (op_high[...], op_low[...]))
    wait_all(share_mid)
    total += product_t(split(whole(mid)), (first_high[...], first_low[...]))
    high, low = split(total)
    op_high[...] = high
    op_low[...] = low
    wait_all(share_inv0)
    put(0, w_part[0] - product_t(split(whole(inv0)), (op_high[...], op_low[...])))
    landed0 = reduce_start(0)
    waits1 = reduce_pass(1, landed1)
    done += reduce_end(1, landed1, waits1)
    waits0 = reduce_pass(0, landed0)
    done += reduce_end(0, landed0, waits0)
    wait_all(done)
    for copy in sends:
        copy.wait_send()


def per_device(rhs_sub, rhs_anc, inv_sub, panel_mid, panel_anc, block_mask, inv_anc):
    any_space = pl.BlockSpec(memory_space=pl.ANY)
    vmem = pltpu.VMEM
    return pl.pallas_call(
        kernel,
        out_shape=(
            jax.ShapeDtypeStruct((1, 2, 32, 512), F32),
            jax.ShapeDtypeStruct((512, 512), F32),
        ),
        in_specs=[any_space] * 5 + [pl.BlockSpec(memory_space=pltpu.SMEM), any_space],
        out_specs=(any_space, any_space),
        scratch_shapes=[
            vmem((2, 4, 4, 64, 128), F32),
            vmem((2, 64, 128), F32),
            vmem((4, 4, 2, 2, 16, 1024), F32),
            vmem((4, 4, 2, 2, 16, 1024), F32),
            vmem((4, 4, 2, 2, 16, 1024), F32),
            vmem((2, 2, 512, 1024), F32),
            vmem((2, 512, 1024), F32),
            vmem((2, 512, 256), F32),
            vmem((2, 4, 4, 64, 128), F32),
            vmem((2, 4, 4, 64, 128), F32),
            vmem((1024, 256), BF16),
            vmem((1024, 256), BF16),
            vmem((1024, 256), BF16),
            vmem((1024, 256), BF16),
            vmem((1024, 1024), BF16),
            vmem((1024, 1024), BF16),
            vmem((1024, 1024), BF16),
            vmem((1024, 1024), BF16),
            vmem((4, 256, 256), F32),
            vmem((3, 256, 256), F32),
            vmem((4, 256, 256), F32),
            vmem((2, 512, 256), F32),
            vmem((2, 64, 256), F32),
            vmem((2, 1024, 256), F32),
            vmem((2, 2, 4, 4, 64, 128), F32),
            vmem((2, 2, 3, 4, 64, 128), F32),
            vmem((2, 2, 3, 64, 128), F32),
            vmem((2, 2, 3, 64, 128), F32),
            vmem((2, 64, 256), F32),
            vmem((2, 2, 4, 8, 128), F32),
            pltpu.SemaphoreType.DMA((COPIES,)),
            pltpu.SemaphoreType.DMA((COPIES,)),
            pltpu.SemaphoreType.DMA((32,)),
        ],
        compiler_params=pltpu.CompilerParams(
            collective_id=0, has_side_effects=True, vmem_limit_bytes=60 * 2**20
        ),
        cost_estimate=pl.CostEstimate(flops=3 * 2 * 2900 * 2**20, bytes_accessed=10 * 2**20, transcendentals=0),
        name="solve",
    )(rhs_sub, rhs_anc, inv_sub, panel_mid, panel_anc, block_mask, inv_anc)


def solution(mesh):
    return jax.shard_map(
        per_device,
        mesh=mesh,
        in_specs=(
            P("leaf", None, "row", None),
            P("row", None),
            P("leaf", None, "row", None),
            P("leaf", "row", None),
            P("leaf", None, "row", None),
            P("leaf", None, "row"),
            P("row", None),
        ),
        out_specs=(P("leaf", None, "row", None), P("row", None)),
        check_vma=False,
    )
```

```python
import functools

import jax
import jax.numpy as jnp
from jax import lax
from jax.experimental import pallas as pl
from jax.experimental.pallas import tpu as pltpu
from jax.sharding import PartitionSpec as P

F32 = jnp.float32
BF16 = jnp.bfloat16
MESH = pl.DeviceIdType.MESH
COPIES = 256


def split(value):
    high = value.astype(BF16)
    return high, (value - high.astype(F32)).astype(BF16)


def dot(left, right):
    return jnp.dot(left, right, preferred_element_type=F32)


def product(left, right):
    left_high, left_low = left
    right_high, right_low = right
    return dot(left_high, right_high) + (dot(left_high, right_low) + dot(left_low, right_high))


def product_t(left, right):
    def one(a, b):
        return lax.dot_general(a, b, (((0,), (0,)), ((), ())), preferred_element_type=F32)

    left_high, left_low = left
    right_high, right_low = right
    return one(left_high, right_high) + (one(left_high, right_low) + one(left_low, right_high))


def kernel(
    rhs_sub, rhs_anc, inv_sub, panel_mid, panel_anc, mask, inv_anc,
    x_sub, x_anc,
    rhs0, rhs1, inv0, inv1, mid, panels, anc, anc_rhs,
    first, tee, op_high, op_low, first_high, first_low,
    q_high, q_low, g_high, g_low,
    update, y_in, value, x_out, own,
    w_part, w_send, r_first, r_sum, r_second, out_sub, mask_tile,
    send_sem, recv_sem, local_sem,
):
    y = lax.axis_index("leaf")
    r = lax.axis_index("row")
    x, z, c = r // 8, (r // 2) % 4, r % 2
    o = 1 - c

    def at_x(d):
        return (y, ((x + d) % 4) * 8 + z * 2 + c)

    def at_z(d):
        return (y, x * 8 + ((z + d) % 4) * 2 + c)

    def at_y(d):
        return ((y + d) % 4, r)

    sibling = (y, x * 8 + z * 2 + o)
    ring = (1, 3, 2)

    count = [0, 0]
    sends = []

    def remote(src, dst, landing, device):
        index = count[0]
        count[0] += 1
        out = pltpu.make_async_remote_copy(
            src_ref=src, dst_ref=dst, send_sem=send_sem.at[index], recv_sem=recv_sem.at[index],
            device_id=device, device_id_type=MESH,
        )
        out.start()
        sends.append(out)
        into = pltpu.make_async_remote_copy(
            src_ref=landing, dst_ref=landing, send_sem=send_sem.at[index], recv_sem=recv_sem.at[index],
            device_id=device, device_id_type=MESH,
        )
        return into.wait_recv

    def local(src, dst):
        index = count[1]
        count[1] += 1
        copy = pltpu.make_async_copy(src, dst, local_sem.at[index])
        copy.start()
        return copy.wait

    def wait_all(waits):
        for wait in waits:
            wait()

    def columns(core, half):
        return pl.ds(pl.multiple_of(core * 256 + half * 128, 128), 128)

    def block(i):
        return pl.ds(pl.multiple_of(i * 256, 256), 256)

    mine = pl.ds(pl.multiple_of(c * 32, 32), 32)
    theirs = pl.ds(pl.multiple_of(o * 32, 32), 32)
    both = block(c)
    other = block(o)

    load_rhs0 = [local(rhs_sub.at[0, 0, :, columns(c, h)], rhs0.at[h, x, z, mine]) for h in range(2)]
    load_inv0 = [local(inv_sub.at[0, 0, pl.ds(16 * h, 16)], inv0.at[x, z, c, h]) for h in range(2)]
    load_rhs1 = [local(rhs_sub.at[0, 1, :, columns(c, h)], rhs1.at[h, mine]) for h in range(2)]
    load_inv1 = [local(inv_sub.at[0, 1, pl.ds(16 * h, 16)], inv1.at[x, z, c, h]) for h in range(2)]
    load_mid = [local(panel_mid.at[0, pl.ds(16 * h, 16)], mid.at[x, z, c, h]) for h in range(2)]
    for s in range(2):
        for j in range(4):
            mask_tile[c, s, j] = jnp.full((8, 128), mask[0, s, j].astype(F32), F32)

    barrier = pltpu.get_barrier_semaphore()
    for device in [at_x(1), at_x(2), at_x(3), at_z(1), at_z(2), at_z(3), at_y(1), at_y(2), at_y(3), sibling]:
        pl.semaphore_signal(barrier, inc=1, device_id=device, device_id_type=MESH)
    pl.semaphore_wait(barrier, 10)

    swap_rhs0 = [
        remote(rhs_sub.at[0, 0, :, columns(o, h)], rhs0.at[h, x, z, mine], rhs0.at[h, x, z, theirs], sibling)
        for h in range(2)
    ]

    def vector_start(ref):
        near, far = [[], []], [[], []]
        for d in ring:
            near[0].append(remote(ref.at[0, x, z], ref.at[0, x, z], ref.at[0, x, (z - d) % 4], at_z(d)))
            near[1].append(remote(ref.at[1, x, z], ref.at[1, x, z], ref.at[1, (x - d) % 4, z], at_x(d)))
        for d in ring:
            far[0].append(remote(ref.at[0, x, z], ref.at[0, x, z], ref.at[0, (x - d) % 4, z], at_x(d)))
            far[1].append(remote(ref.at[1, x, z], ref.at[1, x, z], ref.at[1, x, (z - d) % 4], at_z(d)))
        return near, far

    def vector_pass(ref, waits):
        near, far = waits
        for n, e in enumerate(ring):
            k = (z - e) % 4
            near[0][n]()
            for d in ring:
                far[0].append(remote(ref.at[0, x, k], ref.at[0, x, k], ref.at[0, (x - d) % 4, k], at_x(d)))
            k = (x - e) % 4
            near[1][n]()
            for d in ring:
                far[1].append(remote(ref.at[1, k, z], ref.at[1, k, z], ref.at[1, k, (z - d) % 4], at_z(d)))
        return far

    def vector_end(ref, far, high_ref, low_ref):
        for h in range(2):
            wait_all(far[h])
            high, low = split(ref[h].reshape(1024, 128))
            high_ref[:, 128 * h:128 * h + 128] = high
            low_ref[:, 128 * h:128 * h + 128] = low

    def matrix_share(ref):
        return [remote(ref.at[x, z, c], ref.at[x, z, c], ref.at[x, z, o], sibling)]

    def matrix_start(ref):
        near = [[], []]
        for d in ring:
            near[0].append(remote(ref.at[x, z, c, 0], ref.at[x, z, c, 0], ref.at[x, (z - d) % 4, c, 0], at_z(d)))
            near[1].append(remote(ref.at[x, z, c, 1], ref.at[x, z, c, 1], ref.at[(x - d) % 4, z, c, 1], at_x(d)))
        return near

    def matrix_near(ref, near):
        shared = []
        for n, d in enumerate(ring):
            near[0][n]()
            near[1][n]()
            k = (z - d) % 4
            shared.append(remote(ref.at[x, k, c, 0], ref.at[x, k, c, 0], ref.at[x, k, o, 0], sibling))
            k = (x - d) % 4
            shared.append(remote(ref.at[k, z, c, 1], ref.at[k, z, c, 1], ref.at[k, z, o, 1], sibling))
        return shared

    def matrix_far(ref, distances):
        far = []
        for d in distances:
            k = (x - d) % 4
            far.append((d, 0, remote(ref.at[x, :, c, 0], ref.at[x, :, c, 0], ref.at[k, :, c, 0], at_x(d))))
            k = (z - d) % 4
            far.append((d, 1, remote(ref.at[:, z, c, 1], ref.at[:, z, c, 1], ref.at[:, k, c, 1], at_z(d))))
        return far

    def matrix_end(ref, far):
        shared = []
        for d, h, wait in far:
            wait()
            if h == 0:
                k = (x - d) % 4
                shared.append(remote(ref.at[k, :, c, 0], ref.at[k, :, c, 0], ref.at[k, :, o, 0], sibling))
            else:
                k = (z - d) % 4
                shared.append(remote(ref.at[:, k, c, 1], ref.at[:, k, c, 1], ref.at[:, k, o, 1], sibling))
        return shared

    def masked(s):
        for core in range(2):
            for j in range(4):
                scale = mask_tile[core, s, j][0:1, 0:1]
                panels[s, core, 128 * j:128 * j + 128] = panels[s, core, 128 * j:128 * j + 128] * scale

    def panel(s):
        return panels[s].reshape(1024, 1024)

    def whole(ref):
        return ref[...].reshape(1024, 1024)

    def chip_rows(ref):
        return split(ref[x, z].reshape(64, 1024))

    wait_all(load_rhs0)
    wait_all(swap_rhs0)
    gather0 = vector_start(rhs0)
    wait_all(load_inv0)
    share_inv0 = matrix_share(inv0)
    swap_rhs1 = [
        remote(rhs_sub.at[0, 1, :, columns(o, h)], rhs1.at[h, mine], rhs1.at[h, theirs], sibling)
        for h in range(2)
    ]
    swap_mask = [remote(mask_tile.at[c], mask_tile.at[c], mask_tile.at[o], sibling)]
    wait_all(load_mid)
    share_mid = matrix_share(mid)
    wait_all(load_inv1)
    share_inv1 = matrix_share(inv1)
    gather0 = vector_pass(rhs0, gather0)
    near_inv1 = matrix_start(inv1)
    load_anc = [local(inv_anc, anc.at[c])]
    swap_anc = [remote(inv_anc, anc.at[c], anc.at[o], sibling)]
    load_panels = [local(panel_anc.at[0, s], panels.at[s, c]) for s in range(2)]
    swap_panels = [remote(panel_anc.at[0, s], panels.at[s, c], panels.at[s, o], sibling) for s in range(2)]
    load_anc_rhs = [local(rhs_anc.at[:, both], anc_rhs.at[c])]
    swap_anc_rhs = [remote(rhs_anc.at[:, other], anc_rhs.at[c], anc_rhs.at[o], sibling)]
    wait_all(share_inv0)
    vector_end(rhs0, gather0, op_high, op_low)
    got = product(chip_rows(inv0), (op_high[...], op_low[...]))
    own[0] = got
    for h in range(2):
        first[h, x, z] = got[:, 128 * h:128 * h + 128]
    gather1 = vector_start(first)
    share_inv1 += matrix_near(inv1, near_inv1)
    gather1 = vector_pass(first, gather1)
    far_inv1 = matrix_far(inv1, (1, 3))
    wait_all(load_anc)
    wait_all(swap_anc)
    for n in range(4):
        cols = slice(256 * n, 256 * n + 256)
        high, low = split(product_t(split(whole(anc)), split(anc[:, :, cols].reshape(1024, 256))))
        g_high[:, cols] = high
        g_low[:, cols] = low
    wait_all(load_rhs1)
    wait_all(swap_rhs1)
    wait_all(share_mid)
    vector_end(first, gather1, first_high, first_low)
    got = product(chip_rows(mid), (first_high[...], first_low[...]))
    for h in range(2):
        tee[h, x, z] = rhs1[h] - got[:, 128 * h:128 * h + 128]
    gather2 = vector_start(tee)
    far_inv1 += matrix_far(inv1, (2,))
    gather2 = vector_pass(tee, gather2)
    wait_all(swap_mask)
    wait_all(load_panels)
    wait_all(swap_panels)
    masked(0)
    update[...] = product(split(panel(0)), (first_high[...], first_low[...])).reshape(4, 256, 256)
    masked(1)
    share_inv1 += matrix_end(inv1, far_inv1)
    wait_all(share_inv1)
    near_inv0 = matrix_start(inv0)
    near_mid = matrix_start(mid)
    for n in range(4):
        cols = slice(256 * n, 256 * n + 256)
        below = inv1[n:, :, :, :, :, cols].reshape(1024 - 256 * n, 256)
        left = panels[1, :, :, 256 * n:].reshape(1024, 1024 - 256 * n)
        high, low = split(product(split(left), split(below)))
        q_high[:, cols] = high
        q_low[:, cols] = low
    vector_end(tee, gather2, op_high, op_low)

    def update_block(i):
        rows = block(i)
        update[i] = update[i] + product((q_high[rows], q_low[rows]), (op_high[...], op_low[...]))

    update_in = []
    for d in ring:
        k = (y + d) % 4
        update_block(k)
        update_in.append(remote(update.at[k], y_in.at[d - 1], y_in.at[d - 1], at_y(d)))
    update_block(y)
    share_inv0 = matrix_near(inv0, near_inv0)
    far_inv0 = matrix_far(inv0, ring)
    share_mid = matrix_near(mid, near_mid)
    far_mid = matrix_far(mid, ring)
    own[1] = product(chip_rows(inv1), (op_high[...], op_low[...]))
    for s, ref in enumerate((inv0, inv1)):
        w_part[s] = product_t(chip_rows(ref), split(own[s]))
    wait_all(load_anc_rhs)
    wait_all(swap_anc_rhs)
    wait_all(update_in)
    rows = block(y % 2)
    value[y] = anc_rhs[y // 2, rows] - ((update[y] + y_in[0]) + (y_in[1] + y_in[2]))
    value_in = [remote(value.at[y], value.at[y], value.at[(y - d) % 4], at_y(d)) for d in ring]
    share_inv0 += matrix_end(inv0, far_inv0)

    def solve_part(i):
        cols = block(i)
        return product((g_high[:, cols], g_low[:, cols]), split(value[i])).reshape(2, 512, 256)

    x_out[...] = solve_part(y)
    share_mid += matrix_end(mid, far_mid)
    for n, d in enumerate(ring):
        value_in[n]()
        x_out[...] += solve_part((y - d) % 4)
    high, low = split(x_out[...].reshape(1024, 256))
    op_high[...] = high
    op_low[...] = low

    def reduce_start(s):
        landed = {}
        for e in (2, 1, 3, 0):
            k = (z + e) % 4
            landed[0, e] = [
                remote(w_send.at[s, 0, (x + d) % 4, k], r_first.at[s, 0, d - 1, k], r_first.at[s, 0, d - 1, k], at_x(d))
                for d in ring
            ]
            k = (x + e) % 4
            landed[1, e] = [
                remote(w_send.at[s, 1, k, (z + d) % 4], r_first.at[s, 1, d - 1, k], r_first.at[s, 1, d - 1, k], at_z(d))
                for d in ring
            ]
        return landed

    def reduce_sum(s, landed, h, e):
        wait_all(landed[h, e])
        k = ((z if h == 0 else x) + e) % 4
        kept = w_send[s, 0, x, k] if h == 0 else w_send[s, 1, k, z]
        return (kept + r_first[s, h, 0, k]) + (r_first[s, h, 1, k] + r_first[s, h, 2, k])

    def reduce_pass(s, landed):
        waits = [[], []]
        for e in (2, 1, 3):
            for h in range(2):
                r_sum[s, h, e - 1] = reduce_sum(s, landed, h, e)
                device = at_z(e) if h == 0 else at_x(e)
                waits[h].append(
                    remote(r_sum.at[s, h, e - 1], r_second.at[s, h, e - 1], r_second.at[s, h, e - 1], device)
                )
        return waits

    def reduce_end(s, landed, waits):
        for h in range(2):
            total = reduce_sum(s, landed, h, 0)
            wait_all(waits[h])
            total += r_second[s, h, 0] + (r_second[s, h, 1] + r_second[s, h, 2])
            out_sub[s, :, 128 * h:128 * h + 128] = total
        out = remote(out_sub.at[s, theirs], x_sub.at[0, s, :, both], x_sub.at[0, s, :, other], sibling)
        return [out, local(out_sub.at[s, mine], x_sub.at[0, s, :, both])]

    def put(s, total):
        for h in range(2):
            w_send[s, h] = total[:, 128 * h:128 * h + 128].reshape(4, 4, 64, 128)

    total = w_part[1] - product_t((q_high[...], q_low[...]), (op_high[...], op_low[...]))
    put(1, total)
    landed1 = reduce_start(1)
    high, low = split(total)
    first_high[...] = high
    first_low[...] = low
    done = [remote(x_out.at[o], x_anc.at[:, both], x_anc.at[:, other], sibling)]
    done.append(local(x_out.at[c], x_anc.at[:, both]))
    total = product_t(split(panel(0)), (op_high[...], op_low[...]))
    wait_all(share_mid)
    total += product_t(split(whole(mid)), (first_high[...], first_low[...]))
    high, low = split(total)
    op_high[...] = high
    op_low[...] = low
    wait_all(share_inv0)
    put(0, w_part[0] - product_t(split(whole(inv0)), (op_high[...], op_low[...])))
    landed0 = reduce_start(0)
    waits1 = reduce_pass(1, landed1)
    done += reduce_end(1, landed1, waits1)
    waits0 = reduce_pass(0, landed0)
    done += reduce_end(0, landed0, waits0)
    wait_all(done)
    for copy in sends:
        copy.wait_send()


def per_device(rhs_sub, rhs_anc, inv_sub, panel_mid, panel_anc, block_mask, inv_anc):
    any_space = pl.BlockSpec(memory_space=pl.ANY)
    vmem = pltpu.VMEM
    return pl.pallas_call(
        kernel,
        out_shape=(
            jax.ShapeDtypeStruct((1, 2, 32, 512), F32),
            jax.ShapeDtypeStruct((512, 512), F32),
        ),
        in_specs=[any_space] * 5 + [pl.BlockSpec(memory_space=pltpu.SMEM), any_space],
        out_specs=(any_space, any_space),
        scratch_shapes=[
            vmem((2, 4, 4, 64, 128), F32),
            vmem((2, 64, 128), F32),
            vmem((4, 4, 2, 2, 16, 1024), F32),
            vmem((4, 4, 2, 2, 16, 1024), F32),
            vmem((4, 4, 2, 2, 16, 1024), F32),
            vmem((2, 2, 512, 1024), F32),
            vmem((2, 512, 1024), F32),
            vmem((2, 512, 256), F32),
            vmem((2, 4, 4, 64, 128), F32),
            vmem((2, 4, 4, 64, 128), F32),
            vmem((1024, 256), BF16),
            vmem((1024, 256), BF16),
            vmem((1024, 256), BF16),
            vmem((1024, 256), BF16),
            vmem((1024, 1024), BF16),
            vmem((1024, 1024), BF16),
            vmem((1024, 1024), BF16),
            vmem((1024, 1024), BF16),
            vmem((4, 256, 256), F32),
            vmem((3, 256, 256), F32),
            vmem((4, 256, 256), F32),
            vmem((2, 512, 256), F32),
            vmem((2, 64, 256), F32),
            vmem((2, 1024, 256), F32),
            vmem((2, 2, 4, 4, 64, 128), F32),
            vmem((2, 2, 3, 4, 64, 128), F32),
            vmem((2, 2, 3, 64, 128), F32),
            vmem((2, 2, 3, 64, 128), F32),
            vmem((2, 64, 256), F32),
            vmem((2, 2, 4, 8, 128), F32),
            pltpu.SemaphoreType.DMA((COPIES,)),
            pltpu.SemaphoreType.DMA((COPIES,)),
            pltpu.SemaphoreType.DMA((32,)),
        ],
        compiler_params=pltpu.CompilerParams(
            collective_id=0, has_side_effects=True, vmem_limit_bytes=60 * 2**20
        ),
        cost_estimate=pl.CostEstimate(flops=3 * 2 * 2900 * 2**20, bytes_accessed=10 * 2**20, transcendentals=0),
        name="solve",
    )(rhs_sub, rhs_anc, inv_sub, panel_mid, panel_anc, block_mask, inv_anc)


def solution(mesh):
    return jax.shard_map(
        per_device,
        mesh=mesh,
        in_specs=(
            P("leaf", None, "row", None),
            P("row", None),
            P("leaf", None, "row", None),
            P("leaf", "row", None),
            P("leaf", None, "row", None),
            P("leaf", None, "row"),
            P("row", None),
        ),
        out_specs=(P("leaf", None, "row", None), P("row", None)),
        check_vma=False,
    )
```
